32 devices in a mesh: replica: 8 (over z, y), weight: 4 (over x, core).
Axes of the slice: x: 2, y: 2, z: 4, core: 2. Of those that a mesh axis runs over, the one named last changes fastest.
Arguments:
- images: bfloat16 [512, 14, 14, 512], P(('replica', 'weight')), may hold values from -6 to 6
- gains: bfloat16 [2, 512], P(None, 'weight'), may hold values from 0.5 to 1.5
- biases: bfloat16 [6, 512], P(None, 'weight'), may hold values from -2 to 2
- qkv_weight: bfloat16 [512, 1536], P('weight'), may hold values from -0.25 to 0.25
- bias_table: bfloat16 [169, 16], P(None, 'weight'), may hold values from -4 to 4
- proj_weight: bfloat16 [512, 512], P('weight'), may hold values from -2 to 2
- fc1_weight: bfloat16 [512, 2048], P('weight'), may hold values from -0.25 to 0.25
- fc1_bias: bfloat16 [2048], P('weight'), may hold values from -2 to 2
- fc2_weight: bfloat16 [2048, 512], P('weight'), may hold values from -0.125 to 0.125
- rel_index: int32 [49, 49], replicated, may hold values from 0 to 168, as said below
- cotangent: bfloat16 [512, 14, 14, 512], P(('replica', 'weight')), may hold values from -6 to 6
Outputs:
- output: bfloat16 [512, 14, 14, 512], P(('replica', 'weight'))
- input_grad: bfloat16 [512, 14, 14, 512], P(('replica', 'weight'))
- gains_grad: float32 [2, 512], P(None, 'weight')
- biases_grad: float32 [6, 512], P(None, 'weight')
- qkv_grad: float32 [512, 1536], P('weight')
- table_grad: float32 [169, 16], P(None, 'weight')
- proj_grad: float32 [512, 512], P('weight')
- fc1_grad: float32 [512, 2048], P('weight')
- fc1_bias_grad: float32 [2048], P('weight')
- fc2_grad: float32 [2048, 512], P('weight')
The draws below stay inside these ranges and needn't reach their ends.
Inputs may be any that keep to these rules, and one draw needn't show every extreme that they name: `rel_index`: entries of two query and key pairs hold the same value exactly when the pairs have the same relative offset within a window; all (7*2-1)^2 values occur.
All inputs are finite; a program needn't handle non-finite values.
Results may differ from the reference program's by a relative error of at most 0.013.
Values may be sent and summed in bfloat16 or wider, within the bound.
A program may use at most 320 MiB of HBM per device.

```python
import jax
import jax.numpy as jnp
from jax import lax

D = 512
HEADS = 16
FF = 2048
GRID = 14
WIN = 7
SHIFT = 3
IMAGES = 512


def draw_rel_index(key, part):
    key = jax.random.fold_in(key, 7)
    span_size = 2 * WIN - 1
    ordering = jax.random.permutation(key, span_size * span_size).astype(jnp.int32)
    places = jnp.arange(WIN * WIN, dtype=jnp.int32)
    row_pos = places // WIN
    col_pos = places % WIN
    offsets = (row_pos[:, None] - row_pos[None, :] + WIN - 1) * span_size + (col_pos[:, None] - col_pos[None, :] + WIN - 1)
    return ordering[offsets]


def shard_levels(stream_key, dims, cuts, smallest, top_value):
    loudness = 1.0
    for axis_at, shards_of in cuts:
        heights = jax.random.uniform(jax.random.fold_in(jax.random.fold_in(stream_key, 6), axis_at), (shards_of,), jnp.float32, smallest / len(cuts), top_value / len(cuts))
        loudness = loudness * jnp.repeat(jnp.exp(heights), dims[axis_at] // shards_of).reshape((-1,) + (1,) * (len(dims) - 1 - axis_at))
    return loudness


def bell_draw(rng, dims, scale, reach, cuts=(), kind=jnp.bfloat16):
    array = scale * jax.random.normal(rng, dims, jnp.float32)
    if cuts:
        array = array * shard_levels(rng, dims, cuts, -0.22, 0.18)
    return jnp.clip(array, -reach, reach).astype(kind)


def setup_inputs(seed: int = 0) -> dict:
    keys = jax.random.split(jax.random.key(seed), 12)
    images = bell_draw(keys[0], (IMAGES, GRID, GRID, D), 1.0, 6.0, ((0, 32),))
    gains = jnp.clip(1.0 + 0.1 * jax.random.normal(keys[1], (2, D), jnp.float32), 0.5, 1.5).astype(jnp.bfloat16)
    biases = bell_draw(keys[2], (6, D), 0.3, 2.0, ((1, 4),))
    qkv_weight = bell_draw(keys[3], (D, 3 * D), D ** -0.5, 0.25, ((0, 4),))
    bias_table = bell_draw(keys[4], ((2 * WIN - 1) ** 2, HEADS), 1.0, 4.0, ((1, 4),))
    proj_weight = bell_draw(keys[5], (D, D), (max(D // 49, 1)) ** -0.5, 2.0, ((0, 4),))
    fc1_weight = bell_draw(keys[6], (D, FF), D ** -0.5, 0.25, ((0, 4),))
    fc1_bias = bell_draw(keys[7], (FF,), 0.3, 2.0, ((0, 4),))
    fc2_weight = bell_draw(keys[8], (FF, D), FF ** -0.5, 0.125, ((0, 4),))
    rel_index = draw_rel_index(jax.random.fold_in(keys[11], 71), 0)
    cotangent = bell_draw(keys[10], (IMAGES, GRID, GRID, D), 1.0, 6.0, ((0, 32),))
    return dict(images=images, gains=gains, biases=biases, qkv_weight=qkv_weight, bias_table=bias_table, proj_weight=proj_weight, fc1_weight=fc1_weight, fc1_bias=fc1_bias, fc2_weight=fc2_weight, rel_index=rel_index, cotangent=cotangent)


epsilon = 1e-05
highest = lax.Precision.HIGHEST

@jax.custom_vjp
def low(v):
    return lax.optimization_barrier(v.astype(jnp.bfloat16)).astype(jnp.float32)

@jax.custom_vjp
def low_back(v):
    return v

def low_keep(v):
    return (low(v), None)

def low_pass(kept, grad):
    return (grad,)

def back_keep(v):
    return (v, None)

def back_low(kept, grad):
    return (low(grad),)
low.defvjp(low_keep, low_pass)
low_back.defvjp(back_keep, back_low)

def layer_norm(values, gain, offset):
    center = values - lax.optimization_barrier(jnp.mean(values, axis=-1, keepdims=True))
    spread = lax.optimization_barrier(jnp.mean(center * center, axis=-1, keepdims=True))
    return center * lax.rsqrt(spread + epsilon) * gain + offset

def to_windows(pictures):
    number = pictures.shape[0]
    across = GRID // WIN
    tiles = pictures.reshape(number, across, WIN, across, WIN, pictures.shape[-1])
    return tiles.transpose(0, 1, 3, 2, 4, 5).reshape(number * across * across, WIN * WIN, pictures.shape[-1])

def from_windows(windows):
    across = GRID // WIN
    number = windows.shape[0] // (across * across)
    tiles = windows.reshape(number, across, across, WIN, WIN, windows.shape[-1])
    return tiles.transpose(0, 1, 3, 2, 4, 5).reshape(number, GRID, GRID, windows.shape[-1])

def region_mask():
    places = jnp.arange(GRID, dtype=jnp.int32)
    bands = (places >= GRID - WIN).astype(jnp.int32) + (places >= GRID - SHIFT).astype(jnp.int32)
    labels = bands[:, None] * 3 + bands[None, :]
    across = GRID // WIN
    labels = labels.reshape(across, WIN, across, WIN).transpose(0, 2, 1, 3).reshape(across * across, WIN * WIN)
    return jnp.where(labels[:, :, None] == labels[:, None, :], 0.0, -100.0).astype(jnp.float32)

def one_hot_index(rel_index):
    entries = jnp.arange((2 * WIN - 1) ** 2, dtype=jnp.int32)
    return (rel_index.reshape(-1)[:, None] == entries[None, :]).astype(jnp.float32)

def block_group(window_in, params, table_hot, mask_tiled):
    gains, biases, qkv_weight, bias_table, proj_weight, fc1_weight, fc1_bias, fc2_weight = params
    number, length, width = window_in.shape
    heads = bias_table.shape[1]
    size_head = width // heads
    scale = size_head ** (-0.5)
    normed = low(layer_norm(window_in, gains[0], biases[0]))
    qkv_bias = jnp.concatenate([biases[2], jnp.zeros_like(biases[2]), biases[3]])
    mixed = jnp.einsum('wld,de->wle', normed, qkv_weight, precision=highest) + qkv_bias
    mixed = low(low_back(mixed)).reshape(number, length, 3, heads, size_head)
    queries = mixed[:, :, 0]
    keys_all = mixed[:, :, 1]
    values_all = mixed[:, :, 2]
    rel_bias = jnp.dot(table_hot, bias_table, precision=highest).reshape(length, length, heads).transpose(2, 0, 1)
    scores = scale * jnp.einsum('wqhe,wkhe->whqk', queries, keys_all, precision=highest)
    scores = low_back(scores + rel_bias[None] + mask_tiled[:, None])
    probs = low(jax.nn.softmax(scores, axis=-1))
    attended = jnp.einsum('whqk,wkhe->wqhe', probs, values_all, precision=highest).reshape(number, length, width)
    attended = low(low_back(attended))
    branch = low_back(jnp.einsum('wld,de->wle', attended, proj_weight, precision=highest) + biases[4])
    middle = window_in + branch
    normed_two = low(layer_norm(middle, gains[1], biases[1]))
    hidden = low_back(jnp.einsum('wld,df->wlf', normed_two, fc1_weight, precision=highest) + fc1_bias)
    activated = low(jax.nn.gelu(hidden, approximate=False))
    mlp_out = low_back(jnp.einsum('wlf,fd->wld', activated, fc2_weight, precision=highest) + biases[5])
    return middle + mlp_out

def reference(images, gains, biases, qkv_weight, bias_table, proj_weight, fc1_weight, fc1_bias, fc2_weight, rel_index, cotangent):
    params = tuple((weight.astype(jnp.float32) for weight in (gains, biases, qkv_weight, bias_table, proj_weight, fc1_weight, fc1_bias, fc2_weight)))
    table_hot = one_hot_index(rel_index)
    per_step = 16
    mask_tiled = jnp.tile(region_mask(), (per_step, 1, 1))

    def forward(inputs, weights):
        shifted = jnp.roll(inputs, (-SHIFT, -SHIFT), (1, 2))
        stacked = shifted.reshape(-1, per_step, GRID, GRID, D)

        def one_group(batch_images):
            return from_windows(block_group(to_windows(batch_images), weights, table_hot, mask_tiled))
        outputs = lax.map(jax.checkpoint(one_group), stacked)
        return jnp.roll(outputs.reshape(inputs.shape), (SHIFT, SHIFT), (1, 2))
    result, pullback = jax.vjp(forward, images.astype(jnp.float32), params)
    input_grad, weight_grads = pullback(cotangent.astype(jnp.float32))
    return (result.astype(jnp.bfloat16), input_grad.astype(jnp.bfloat16), weight_grads[0], weight_grads[1], weight_grads[2], weight_grads[3], weight_grads[4], weight_grads[5], weight_grads[6], weight_grads[7])
```

```python
import functools

import jax
import jax.numpy as jnp
import numpy as np
from jax import lax
from jax.experimental import pallas as pl
from jax.experimental.pallas import tpu as pltpu
from jax.sharding import PartitionSpec as P

GRID = 14
WIN = 7
SHIFT = 3
ACROSS = GRID // WIN
LEN = WIN * WIN
SLOT = 56
ROWS = ACROSS * ACROSS * SLOT
LINE = 16
SPAN = (2 * WIN - 1) ** 2
GROUP = 4
BATCH = 2
F32 = jnp.float32
BF16 = jnp.bfloat16
EPSILON = 1e-05


def token_permutation():
    matrix = np.zeros((ROWS, GRID * LINE), np.float32)
    for w in range(ACROSS * ACROSS):
        for i in range(LEN):
            row = ((w // ACROSS) * WIN + i // WIN + SHIFT) % GRID
            col = ((w % ACROSS) * WIN + i % WIN + SHIFT) % GRID
            matrix[w * SLOT + i, row * LINE + col] = 1.0
    return matrix


def region_mask():
    places = np.arange(GRID)
    bands = (places >= GRID - WIN).astype(np.int32) + (places >= GRID - SHIFT).astype(np.int32)
    labels = bands[:, None] * 3 + bands[None, :]
    labels = (
        labels.reshape(ACROSS, WIN, ACROSS, WIN)
        .transpose(0, 2, 1, 3)
        .reshape(ACROSS * ACROSS, LEN)
    )
    mask = np.zeros((ACROSS * ACROSS, SLOT, SLOT), np.float32)
    mask[:, :LEN, :LEN] = np.where(labels[:, :, None] == labels[:, None, :], 0.0, -100.0)
    mask[:, LEN:, :] = -1e30
    return mask


def dot(a, b):
    return jnp.dot(a, b, preferred_element_type=F32)


def dot_t(a, b):
    return lax.dot_general(a, b, (((1,), (1,)), ((), ())), preferred_element_type=F32)


def t_dot(a, b):
    return lax.dot_general(a, b, (((0,), (0,)), ((), ())), preferred_element_type=F32)


def normalise(values):
    center = values - jnp.mean(values, axis=-1, keepdims=True)
    spread = jnp.mean(center * center, axis=-1, keepdims=True)
    inverse = lax.rsqrt(spread + EPSILON)
    return center * inverse, inverse


def norm_back(grad, unit, inverse, gain):
    scaled = grad * gain
    return inverse * (
        scaled
        - jnp.mean(scaled, axis=-1, keepdims=True)
        - unit * jnp.mean(scaled * unit, axis=-1, keepdims=True)
    )


def column_sum(values):
    return jnp.sum(values, axis=0, keepdims=True)


def gelu_parts(hidden):
    bell = jnp.exp(hidden * hidden * -0.5)
    step = 1.0 / (1.0 + (0.3275911 * 0.7071067811865476) * jnp.abs(hidden))
    series = step * (
        0.5 * 0.254829592
        + step
        * (
            0.5 * -0.284496736
            + step * (0.5 * 1.421413741 + step * (0.5 * -1.453152027 + step * (0.5 * 1.061405429)))
        )
    )
    tail = series * bell
    below = jnp.where(hidden < 0.0, tail, 1.0 - tail)
    return below, bell * 0.3989422804014327


def head_masks(width_head):
    lanes = lax.broadcasted_iota(jnp.int32, (SLOT, GROUP * width_head), 1)
    return [
        (lanes >= h * width_head) & (lanes < (h + 1) * width_head) for h in range(GROUP)
    ]


def expand(block, masks):
    return jnp.concatenate([jnp.where(m, block, 0.0) for m in masks], axis=0).astype(BF16)


def collect(rows, masks):
    total = jnp.where(masks[0], rows[:SLOT], 0.0)
    for h in range(1, GROUP):
        total = jnp.where(masks[h], rows[h * SLOT : (h + 1) * SLOT], total)
    return total


def read_image(ref, at, grid_ref, perm_ref):
    for r in range(GRID):
        grid_ref[r * LINE : r * LINE + GRID, :] = ref[at, r]
    return dot(perm_ref[...], grid_ref[...])


def write_image(ref, at, values, back_ref):
    lines = dot(back_ref[...], values).astype(BF16)
    for r in range(GRID):
        ref[at, r] = lines[r * LINE : r * LINE + GRID]


def forward_kernel(
    width_head,
    images, cotangent, weights, reduce, vectors, qkv_bias, expand_bias, rel_bias, mask, perm, back,
    output, mixed_out, attended_out, middle_out, probs_out, expand_grad, reduce_grad, sums, expand_sums,
    grid_rows, inputs, ups, mixed, attended, expand_acc, reduce_acc,
):
    width = inputs.shape[1]
    hidden_width = expand_bias.shape[1]
    step = pl.program_id(0)

    @pl.when(step == 0)
    def _():
        grid_rows[...] = jnp.zeros_like(grid_rows)
        expand_acc[...] = jnp.zeros_like(expand_acc)
        reduce_acc[...] = jnp.zeros_like(reduce_acc)
        sums[...] = jnp.zeros_like(sums)
        expand_sums[...] = jnp.zeros_like(expand_sums)

    for b in range(BATCH):
        inputs[b * ROWS : (b + 1) * ROWS, :] = read_image(images, b, grid_rows, perm)
        ups[b * ROWS : (b + 1) * ROWS, :] = read_image(cotangent, b, grid_rows, perm)
    unit, _ = normalise(inputs[...])
    normed = (unit * vectors[0:1, :] + vectors[2:3, :]).astype(BF16)
    mixed_low = (dot(normed, weights[:, : 3 * width]) + qkv_bias[...]).astype(BF16)
    mixed_out[...] = mixed_low
    mixed[...] = mixed_low.astype(F32)
    scale = width_head ** (-0.5)

    def attend(w, carry):
        masks = head_masks(width_head)
        rows = pl.ds(pl.multiple_of(w * SLOT, 8), SLOT)
        region = mask[lax.rem(w, ACROSS * ACROSS)]
        size = GROUP * width_head
        for g in range(width // size):
            queries = mixed[rows, g * size : (g + 1) * size].astype(BF16)
            keys = expand(mixed[rows, width + g * size : width + (g + 1) * size], masks)
            values = expand(mixed[rows, 2 * width + g * size : 2 * width + (g + 1) * size], masks)
            scores = dot_t(keys, queries) * scale + rel_bias[g]
            scores = scores.reshape(GROUP, SLOT, SLOT) + region[None]
            raised = jnp.exp(scores - jnp.max(scores, axis=1, keepdims=True))
            probs = raised * (1.0 / jnp.sum(raised, axis=1, keepdims=True))
            probs = probs.reshape(GROUP * SLOT, SLOT).astype(BF16)
            probs_out[w * (width // size) + g] = probs
            attended[rows, g * size : (g + 1) * size] = t_dot(probs, values)
        return carry

    lax.fori_loop(0, BATCH * ACROSS * ACROSS, attend, 0)

    attended_low = attended[...].astype(BF16)
    attended_out[...] = attended_low
    middle = inputs[...] + dot(attended_low, weights[:, 3 * width : 4 * width]) + vectors[6:7, :]
    unit, inverse = normalise(middle)
    normed_two = (unit * vectors[1:2, :] + vectors[3:4, :]).astype(BF16)
    up = ups[...]
    up_low = up.astype(BF16)
    final = middle + vectors[7:8, :]
    grad_normed = jnp.zeros_like(final)
    chunk = 512
    for c in range(hidden_width // chunk):
        part = slice(c * chunk, (c + 1) * chunk)
        expand_part = weights[:, 4 * width + c * chunk : 4 * width + (c + 1) * chunk]
        hidden = dot(normed_two, expand_part) + expand_bias[:, part]
        below, density = gelu_parts(hidden)
        activated = (hidden * below).astype(BF16)
        final = final + dot(activated, reduce[part, :])
        grad_act = dot_t(up_low, reduce[part, :])
        grad_hidden = (grad_act * (below + hidden * density)).astype(BF16)
        expand_sums[:, part] += column_sum(grad_hidden.astype(F32))
        expand_acc[:, part] += t_dot(normed_two, grad_hidden)
        reduce_acc[part, :] += t_dot(activated, up_low)
        grad_normed = grad_normed + dot_t(grad_hidden, expand_part)
    sums[0:1, :] += column_sum(grad_normed * unit)
    sums[1:2, :] += column_sum(grad_normed)
    sums[2:3, :] += column_sum(up)
    middle_out[...] = up + norm_back(grad_normed, unit, inverse, vectors[1:2, :])
    final_low = final.astype(BF16)
    for b in range(BATCH):
        write_image(output, b, final_low[b * ROWS : (b + 1) * ROWS], back)

    @pl.when(step == pl.num_programs(0) - 1)
    def _():
        expand_grad[...] = expand_acc[...].astype(BF16)
        reduce_grad[...] = reduce_acc[...].astype(BF16)


def backward_kernel(
    width_head,
    images, weights, vectors, mixed_in, attended_in, middle_in, probs_in, perm, back,
    input_grad, weight_grad, sums, mixed_sums, rel_grad,
    grid_rows, inputs, mixed, grad_attended, grad_mixed, weight_acc,
):
    width = inputs.shape[1]
    step = pl.program_id(0)

    @pl.when(step == 0)
    def _():
        grid_rows[...] = jnp.zeros_like(grid_rows)
        weight_acc[...] = jnp.zeros_like(weight_acc)
        sums[...] = jnp.zeros_like(sums)
        mixed_sums[...] = jnp.zeros_like(mixed_sums)
        rel_grad[...] = jnp.zeros_like(rel_grad)

    for b in range(BATCH):
        inputs[b * ROWS : (b + 1) * ROWS, :] = read_image(images, b, grid_rows, perm)
    mixed[...] = mixed_in[...].astype(F32)
    middle_low = middle_in[...].astype(BF16)
    weight_acc[:, 3 * width :] += t_dot(attended_in[...], middle_low)
    sums[0:1, :] += column_sum(middle_low.astype(F32))
    grad_attended[...] = dot_t(middle_low, weights[:, 3 * width :]).astype(BF16).astype(F32)
    scale = width_head ** (-0.5)

    def attend(w, carry):
        masks = head_masks(width_head)
        rows = pl.ds(pl.multiple_of(w * SLOT, 8), SLOT)
        size = GROUP * width_head
        for g in range(width // size):
            here = slice(g * size, (g + 1) * size)
            queries = mixed[rows, here].astype(BF16)
            keys = expand(mixed[rows, width + g * size : width + (g + 1) * size], masks)
            values = expand(mixed[rows, 2 * width + g * size : 2 * width + (g + 1) * size], masks)
            grad = grad_attended[rows, here].astype(BF16)
            probs_low = probs_in[w * (width // size) + g]
            probs = probs_low.astype(F32).reshape(GROUP, SLOT, SLOT)
            grad_probs = dot_t(values, grad).reshape(GROUP, SLOT, SLOT)
            grad_values = collect(dot(probs_low, grad), masks)
            shift = jnp.sum(probs * grad_probs, axis=1, keepdims=True)
            grad_scores = (probs * (grad_probs - shift)).reshape(GROUP * SLOT, SLOT).astype(BF16)
            rel_grad[g] += grad_scores.astype(F32)
            grad_mixed[rows, here] = scale * t_dot(grad_scores, keys)
            grad_mixed[rows, width + g * size : width + (g + 1) * size] = scale * collect(
                dot(grad_scores, queries), masks
            )
            grad_mixed[rows, 2 * width + g * size : 2 * width + (g + 1) * size] = grad_values
        return carry

    lax.fori_loop(0, BATCH * ACROSS * ACROSS, attend, 0)

    grad_low = grad_mixed[...].astype(BF16)
    mixed_sums[...] += column_sum(grad_low.astype(F32))
    unit, inverse = normalise(inputs[...])
    normed = (unit * vectors[0:1, :] + vectors[2:3, :]).astype(BF16)
    weight_acc[:, : 3 * width] += t_dot(normed, grad_low)
    grad_normed = dot_t(grad_low, weights[:, : 3 * width])
    sums[1:2, :] += column_sum(grad_normed * unit)
    sums[2:3, :] += column_sum(grad_normed)
    total = middle_in[...] + norm_back(grad_normed, unit, inverse, vectors[0:1, :])
    total_low = total.astype(BF16)
    for b in range(BATCH):
        write_image(input_grad, b, total_low[b * ROWS : (b + 1) * ROWS], back)

    @pl.when(step == pl.num_programs(0) - 1)
    def _():
        weight_grad[...] = weight_acc[...].astype(BF16)


def whole(shape):
    return pl.BlockSpec(shape, lambda i: (0,) * len(shape), pipeline_mode=pl.Buffered(1))


def kept(shape):
    return pl.BlockSpec(shape, lambda i: (0,) * len(shape))


def per_step(*shape):
    return pl.BlockSpec(shape, lambda i: (i,) + (0,) * (len(shape) - 1))


def reduce_owned(grad):
    mine = lax.psum_scatter(grad, "weight", scatter_dimension=0, tiled=True)
    return lax.psum(mine, "replica")


def per_device(
    shards, images, gains, biases, qkv_weight, bias_table, proj_weight, fc1_weight, fc1_bias,
    fc2_weight, rel_index, cotangent,
):
    number, width = images.shape[0], images.shape[-1]
    heads = bias_table.shape[1] * shards
    width_head = width // heads
    hidden_width = fc1_weight.shape[1]
    own = width // shards
    groups = heads // GROUP
    steps = number // BATCH
    rows = BATCH * ROWS
    windows = BATCH * ACROSS * ACROSS

    weights = lax.all_gather(
        jnp.concatenate([qkv_weight, proj_weight, fc1_weight], axis=1), "weight", axis=0, tiled=True
    )
    reduce = lax.all_gather(fc2_weight, "weight", axis=0, tiled=True)
    hidden_lines = hidden_width // shards // own
    table_own = bias_table.T.reshape(-1)
    table_lines = -(-table_own.shape[0] // own)
    table_pad = jnp.pad(table_own, (0, table_lines * own - table_own.shape[0]))
    small = jnp.concatenate(
        [gains, biases, fc1_bias.reshape(hidden_lines, own), table_pad.reshape(table_lines, own)]
    )
    small = lax.all_gather(small, "weight", axis=0)
    vectors = small[:, :8].transpose(1, 0, 2).reshape(8, width).astype(F32)
    expand_bias = small[:, 8 : 8 + hidden_lines].reshape(1, hidden_width).astype(F32)
    table = small[:, 8 + hidden_lines :].reshape(shards, -1)[:, : table_own.shape[0]]
    table = table.reshape(heads, SPAN)
    qkv_bias = jnp.concatenate([vectors[4], jnp.zeros_like(vectors[4]), vectors[5]])[None]

    entries = jnp.arange(SPAN, dtype=jnp.int32)
    hot = (rel_index.T.reshape(-1)[None, :] == entries[:, None]).astype(BF16)
    rel_bias = dot(table, hot).reshape(heads, LEN, LEN)
    rel_bias = jnp.pad(rel_bias, ((0, 0), (0, SLOT - LEN), (0, SLOT - LEN)))
    rel_bias = rel_bias.reshape(groups, GROUP * SLOT, SLOT)
    mask = jnp.asarray(region_mask())
    perm_host = token_permutation()
    perm = jnp.asarray(perm_host, BF16)
    back = jnp.asarray(perm_host.T, BF16)

    image_block = per_step(BATCH, GRID, GRID, width)
    shape = jax.ShapeDtypeStruct
    params = pltpu.CompilerParams(
        dimension_semantics=("arbitrary",), vmem_limit_bytes=60 * 1024 * 1024
    )
    tokens = number * ROWS
    output, mixed, attended, middle, probs, expand_grad, reduce_grad, sums, expand_sums = pl.pallas_call(
        functools.partial(forward_kernel, width_head),
        grid=(steps,),
        in_specs=[
            image_block, image_block, whole(weights.shape), whole(reduce.shape), whole(vectors.shape),
            whole(qkv_bias.shape), whole(expand_bias.shape), whole(rel_bias.shape), whole(mask.shape),
            whole(perm.shape), whole(back.shape),
        ],
        out_specs=[
            image_block, per_step(rows, 3 * width), per_step(rows, width), per_step(rows, width),
            per_step(windows * groups, GROUP * SLOT, SLOT),
            kept((width, hidden_width)), kept((hidden_width, width)), kept((8, width)),
            kept((1, hidden_width)),
        ],
        out_shape=[
            shape(images.shape, BF16), shape((tokens, 3 * width), BF16), shape((tokens, width), BF16),
            shape((tokens, width), F32),
            shape((number * ACROSS * ACROSS * groups, GROUP * SLOT, SLOT), BF16),
            shape((width, hidden_width), BF16), shape((hidden_width, width), BF16),
            shape((8, width), F32), shape((1, hidden_width), F32),
        ],
        scratch_shapes=[
            pltpu.VMEM((GRID * LINE, width), BF16), pltpu.VMEM((rows, width), F32),
            pltpu.VMEM((rows, width), F32), pltpu.VMEM((rows, 3 * width), F32),
            pltpu.VMEM((rows, width), F32), pltpu.VMEM((width, hidden_width), F32),
            pltpu.VMEM((hidden_width, width), F32),
        ],
        compiler_params=params,
        cost_estimate=pl.CostEstimate(flops=50 * 10**9, bytes_accessed=60 * 10**6, transcendentals=0),
    )(images, cotangent, weights, reduce, vectors, qkv_bias, expand_bias, rel_bias, mask, perm, back)

    expand_owned = reduce_owned(expand_grad)
    reduce_owned_grad = reduce_owned(reduce_grad)

    input_grad, weight_grad, sums_two, mixed_sums, rel_grad = pl.pallas_call(
        functools.partial(backward_kernel, width_head),
        grid=(steps,),
        in_specs=[
            image_block, whole((width, 4 * width)), whole(vectors.shape), per_step(rows, 3 * width),
            per_step(rows, width), per_step(rows, width),
            per_step(windows * groups, GROUP * SLOT, SLOT), whole(perm.shape), whole(back.shape),
        ],
        out_specs=[
            image_block, kept((width, 4 * width)), kept((8, width)), kept((1, 3 * width)),
            kept((groups, GROUP * SLOT, SLOT)),
        ],
        out_shape=[
            shape(images.shape, BF16), shape((width, 4 * width), BF16), shape((8, width), F32),
            shape((1, 3 * width), F32), shape((groups, GROUP * SLOT, SLOT), F32),
        ],
        scratch_shapes=[
            pltpu.VMEM((GRID * LINE, width), BF16), pltpu.VMEM((rows, width), F32),
            pltpu.VMEM((rows, 3 * width), F32), pltpu.VMEM((rows, width), F32),
            pltpu.VMEM((rows, 3 * width), F32), pltpu.VMEM((width, 4 * width), F32),
        ],
        compiler_params=params,
        cost_estimate=pl.CostEstimate(flops=30 * 10**9, bytes_accessed=60 * 10**6, transcendentals=0),
    )(images, weights, vectors, mixed, attended, middle, probs, perm, back)

    weight_owned = reduce_owned(weight_grad).astype(F32)

    rel_rows = rel_grad.reshape(heads, SLOT, SLOT)[:, :LEN, :LEN].reshape(heads, LEN * LEN)
    table_grad = lax.dot_general(
        rel_rows, hot.astype(F32), (((1,), (1,)), ((), ())), precision=lax.Precision.HIGHEST
    ).reshape(-1)
    lines = -(-table_grad.shape[0] // width)
    table_grad = jnp.pad(table_grad, (0, lines * width - table_grad.shape[0])).reshape(lines, width)
    mixed_lines = mixed_sums.reshape(3, width)
    packed = jnp.concatenate(
        [
            sums_two[1:2], sums[0:1], sums_two[2:3], sums[1:2], mixed_lines[0:1], mixed_lines[2:3],
            sums_two[0:1], sums[2:3], expand_sums.reshape(hidden_width // width, width), table_grad,
        ]
    )
    packed = lax.psum(packed, ("replica", "weight"))
    mine = lax.axis_index("weight")
    features = lax.dynamic_slice_in_dim(packed[:8], mine * own, own, axis=1)
    hidden_lines = hidden_width // width
    expand_bias_grad = lax.dynamic_slice_in_dim(
        packed[8 : 8 + hidden_lines].reshape(-1), mine * (hidden_width // shards), hidden_width // shards
    )
    table_grad = packed[8 + hidden_lines :].reshape(-1)[: heads * SPAN].reshape(heads, SPAN)
    table_grad = lax.dynamic_slice_in_dim(table_grad, mine * (heads // shards), heads // shards).T
    return (
        output,
        input_grad,
        features[:2],
        features[2:],
        weight_owned[:, : 3 * width],
        table_grad,
        weight_owned[:, 3 * width :],
        expand_owned.astype(F32),
        expand_bias_grad,
        reduce_owned_grad.astype(F32),
    )


def solution(mesh):
    in_specs = (
        P(("replica", "weight"), None, None, None),
        P(None, "weight"),
        P(None, "weight"),
        P("weight", None),
        P(None, "weight"),
        P("weight", None),
        P("weight", None),
        P("weight"),
        P("weight", None),
        P(),
        P(("replica", "weight"), None, None, None),
    )
    out_specs = (
        P(("replica", "weight"), None, None, None),
        P(("replica", "weight"), None, None, None),
        P(None, "weight"),
        P(None, "weight"),
        P("weight", None),
        P(None, "weight"),
        P("weight", None),
        P("weight", None),
        P("weight"),
        P("weight", None),
    )
    return jax.shard_map(
        functools.partial(per_device, mesh.shape["weight"]),
        mesh=mesh,
        in_specs=in_specs,
        out_specs=out_specs,
        check_vma=False,
    )
```

```python
import functools

import jax
import jax.numpy as jnp
import numpy as np
from jax import lax
from jax.experimental import pallas as pl
from jax.experimental.pallas import tpu as pltpu
from jax.sharding import PartitionSpec as P

GRID = 14
WIN = 7
SHIFT = 3
ACROSS = GRID // WIN
LEN = WIN * WIN
SLOT = 56
ROWS = ACROSS * ACROSS * SLOT
LINE = 16
SPAN = (2 * WIN - 1) ** 2
GROUP = 4
BATCH = 2
UNROLL = 2
F32 = jnp.float32
BF16 = jnp.bfloat16
EPSILON = 1e-05


def token_permutation():
    matrix = np.zeros((ROWS, GRID * LINE), np.float32)
    for w in range(ACROSS * ACROSS):
        for i in range(LEN):
            row = ((w // ACROSS) * WIN + i // WIN + SHIFT) % GRID
            col = ((w % ACROSS) * WIN + i % WIN + SHIFT) % GRID
            matrix[w * SLOT + i, row * LINE + col] = 1.0
    return matrix


def region_mask():
    places = np.arange(GRID)
    bands = (places >= GRID - WIN).astype(np.int32) + (places >= GRID - SHIFT).astype(np.int32)
    labels = bands[:, None] * 3 + bands[None, :]
    labels = (
        labels.reshape(ACROSS, WIN, ACROSS, WIN)
        .transpose(0, 2, 1, 3)
        .reshape(ACROSS * ACROSS, LEN)
    )
    mask = np.zeros((ACROSS * ACROSS, SLOT, SLOT), np.float32)
    mask[:, :LEN, :LEN] = np.where(labels[:, :, None] == labels[:, None, :], 0.0, -100.0)
    mask[:, LEN:, :] = -1e30
    return mask


def dot(a, b):
    return jnp.dot(a, b, preferred_element_type=F32)


def dot_t(a, b):
    return lax.dot_general(a, b, (((1,), (1,)), ((), ())), preferred_element_type=F32)


def t_dot(a, b):
    return lax.dot_general(a, b, (((0,), (0,)), ((), ())), preferred_element_type=F32)


def normalise(values):
    center = values - jnp.mean(values, axis=-1, keepdims=True)
    spread = jnp.mean(center * center, axis=-1, keepdims=True)
    inverse = lax.rsqrt(spread + EPSILON)
    return center * inverse, inverse


def norm_back(grad, unit, inverse, gain):
    scaled = grad * gain
    return inverse * (
        scaled
        - jnp.mean(scaled, axis=-1, keepdims=True)
        - unit * jnp.mean(scaled * unit, axis=-1, keepdims=True)
    )


def column_sum(values):
    return jnp.sum(values, axis=0, keepdims=True)


def gelu_parts(hidden):
    bell = jnp.exp(hidden * hidden * -0.5)
    step = 1.0 / (1.0 + (0.3275911 * 0.7071067811865476) * jnp.abs(hidden))
    series = step * (
        0.5 * 0.254829592
        + step
        * (
            0.5 * -0.284496736
            + step * (0.5 * 1.421413741 + step * (0.5 * -1.453152027 + step * (0.5 * 1.061405429)))
        )
    )
    tail = series * bell
    below = jnp.where(hidden < 0.0, tail, 1.0 - tail)
    return below, bell * 0.3989422804014327


def head_masks(width_head):
    lanes = lax.broadcasted_iota(jnp.int32, (SLOT, GROUP * width_head), 1)
    return [
        (lanes >= h * width_head) & (lanes < (h + 1) * width_head) for h in range(GROUP)
    ]


def expand(block, masks):
    return jnp.concatenate([jnp.where(m, block, 0.0) for m in masks], axis=0).astype(BF16)


def collect(rows, masks):
    total = jnp.where(masks[0], rows[:SLOT], 0.0)
    for h in range(1, GROUP):
        total = jnp.where(masks[h], rows[h * SLOT : (h + 1) * SLOT], total)
    return total


def read_image(ref, at, grid_ref, perm_ref):
    for r in range(GRID):
        grid_ref[r * LINE : r * LINE + GRID, :] = ref[at, r]
    return dot(perm_ref[...], grid_ref[...])


def write_image(ref, at, values, back_ref):
    lines = dot(back_ref[...], values).astype(BF16)
    for r in range(GRID):
        ref[at, r] = lines[r * LINE : r * LINE + GRID]


def attention_kernel(
    width_head,
    images, qkv_weight, vectors, qkv_bias, rel_bias, mask, perm,
    mixed_out, attended_out, probs_out,
    grid_rows, inputs, mixed, attended,
):
    width = inputs.shape[1]

    @pl.when(pl.program_id(0) == 0)
    def _():
        grid_rows[...] = jnp.zeros_like(grid_rows)

    for b in range(BATCH):
        inputs[b * ROWS : (b + 1) * ROWS, :] = read_image(images, b, grid_rows, perm)
    unit, _ = normalise(inputs[...])
    normed = (unit * vectors[0:1, :] + vectors[2:3, :]).astype(BF16)
    mixed_low = (dot(normed, qkv_weight[...]) + qkv_bias[...]).astype(BF16)
    mixed_out[...] = mixed_low
    mixed[...] = mixed_low.astype(F32)
    scale = width_head ** (-0.5)

    def attend(w, carry):
        masks = head_masks(width_head)
        rows = pl.ds(pl.multiple_of(w * SLOT, 8), SLOT)
        region = mask[lax.rem(w, ACROSS * ACROSS)]
        size = GROUP * width_head
        for g in range(width // size):
            queries = mixed[rows, g * size : (g + 1) * size].astype(BF16)
            keys = expand(mixed[rows, width + g * size : width + (g + 1) * size], masks)
            values = expand(mixed[rows, 2 * width + g * size : 2 * width + (g + 1) * size], masks)
            scores = dot_t(keys, queries) * scale + rel_bias[g]
            scores = scores.reshape(GROUP, SLOT, SLOT) + region[None]
            raised = jnp.exp(scores - jnp.max(scores, axis=1, keepdims=True))
            probs = raised * (1.0 / jnp.sum(raised, axis=1, keepdims=True))
            probs = probs.reshape(GROUP * SLOT, SLOT).astype(BF16)
            probs_out[w * (width // size) + g] = probs
            attended[rows, g * size : (g + 1) * size] = t_dot(probs, values)
        return carry

    lax.fori_loop(0, BATCH * ACROSS * ACROSS, attend, 0, unroll=UNROLL)
    attended_out[...] = attended[...].astype(BF16)


def mlp_kernel(
    images, cotangent, attended, later, reduce, vectors, expand_bias, perm, back,
    output, middle_out, expand_grad, reduce_grad, sums, expand_sums,
    grid_rows, inputs, ups, expand_acc, reduce_acc,
):
    hidden_width = expand_bias.shape[1]
    step = pl.program_id(0)

    @pl.when(step == 0)
    def _():
        grid_rows[...] = jnp.zeros_like(grid_rows)
        expand_acc[...] = jnp.zeros_like(expand_acc)
        reduce_acc[...] = jnp.zeros_like(reduce_acc)
        sums[...] = jnp.zeros_like(sums)
        expand_sums[...] = jnp.zeros_like(expand_sums)

    for b in range(BATCH):
        inputs[b * ROWS : (b + 1) * ROWS, :] = read_image(images, b, grid_rows, perm)
        ups[b * ROWS : (b + 1) * ROWS, :] = read_image(cotangent, b, grid_rows, perm)
    middle = inputs[...] + dot(attended[...], later[:, hidden_width:]) + vectors[6:7, :]
    unit, inverse = normalise(middle)
    normed_two = (unit * vectors[1:2, :] + vectors[3:4, :]).astype(BF16)
    up = ups[...]
    up_low = up.astype(BF16)
    final = middle + vectors[7:8, :]
    grad_normed = jnp.zeros_like(final)
    chunk = 512
    for c in range(hidden_width // chunk):
        part = slice(c * chunk, (c + 1) * chunk)
        expand_part = later[:, part]
        hidden = dot(normed_two, expand_part) + expand_bias[:, part]
        below, density = gelu_parts(hidden)
        activated = (hidden * below).astype(BF16)
        final = final + dot(activated, reduce[part, :])
        grad_act = dot_t(up_low, reduce[part, :])
        grad_hidden = (grad_act * (below + hidden * density)).astype(BF16)
        expand_sums[:, part] += column_sum(grad_hidden.astype(F32))
        expand_acc[:, part] += t_dot(normed_two, grad_hidden)
        reduce_acc[part, :] += t_dot(activated, up_low)
        grad_normed = grad_normed + dot_t(grad_hidden, expand_part)
    sums[0:1, :] += column_sum(grad_normed * unit)
    sums[1:2, :] += column_sum(grad_normed)
    sums[2:3, :] += column_sum(up)
    middle_out[...] = up + norm_back(grad_normed, unit, inverse, vectors[1:2, :])
    final_low = final.astype(BF16)
    for b in range(BATCH):
        write_image(output, b, final_low[b * ROWS : (b + 1) * ROWS], back)

    @pl.when(step == pl.num_programs(0) - 1)
    def _():
        expand_grad[...] = expand_acc[...].astype(BF16)
        reduce_grad[...] = reduce_acc[...].astype(BF16)


def backward_kernel(
    width_head,
    images, qkv_weight, proj_weight, vectors, mixed_in, attended_in, middle_in, probs_in, perm, back,
    input_grad, weight_grad, sums, mixed_sums, rel_grad,
    grid_rows, inputs, mixed, grad_attended, grad_mixed, weight_acc,
):
    width = inputs.shape[1]
    step = pl.program_id(0)

    @pl.when(step == 0)
    def _():
        grid_rows[...] = jnp.zeros_like(grid_rows)
        weight_acc[...] = jnp.zeros_like(weight_acc)
        sums[...] = jnp.zeros_like(sums)
        mixed_sums[...] = jnp.zeros_like(mixed_sums)
        rel_grad[...] = jnp.zeros_like(rel_grad)

    for b in range(BATCH):
        inputs[b * ROWS : (b + 1) * ROWS, :] = read_image(images, b, grid_rows, perm)
    mixed[...] = mixed_in[...].astype(F32)
    middle_low = middle_in[...].astype(BF16)
    weight_acc[:, 3 * width :] += t_dot(attended_in[...], middle_low)
    sums[0:1, :] += column_sum(middle_low.astype(F32))
    grad_attended[...] = dot_t(middle_low, proj_weight[...]).astype(BF16).astype(F32)
    scale = width_head ** (-0.5)

    def attend(w, carry):
        masks = head_masks(width_head)
        rows = pl.ds(pl.multiple_of(w * SLOT, 8), SLOT)
        size = GROUP * width_head
        for g in range(width // size):
            here = slice(g * size, (g + 1) * size)
            queries = mixed[rows, here].astype(BF16)
            keys = expand(mixed[rows, width + g * size : width + (g + 1) * size], masks)
            values = expand(mixed[rows, 2 * width + g * size : 2 * width + (g + 1) * size], masks)
            grad = grad_attended[rows, here].astype(BF16)
            probs_low = probs_in[w * (width // size) + g]
            probs = probs_low.astype(F32).reshape(GROUP, SLOT, SLOT)
            grad_probs = dot_t(values, grad).reshape(GROUP, SLOT, SLOT)
            grad_values = collect(dot(probs_low, grad), masks)
            shift = jnp.sum(probs * grad_probs, axis=1, keepdims=True)
            grad_scores = (probs * (grad_probs - shift)).reshape(GROUP * SLOT, SLOT).astype(BF16)
            rel_grad[g] += grad_scores.astype(F32)
            grad_mixed[rows, here] = scale * t_dot(grad_scores, keys)
            grad_mixed[rows, width + g * size : width + (g + 1) * size] = scale * collect(
                dot(grad_scores, queries), masks
            )
            grad_mixed[rows, 2 * width + g * size : 2 * width + (g + 1) * size] = grad_values
        return carry

    lax.fori_loop(0, BATCH * ACROSS * ACROSS, attend, 0, unroll=UNROLL)

    grad_low = grad_mixed[...].astype(BF16)
    mixed_sums[...] += column_sum(grad_low.astype(F32))
    unit, inverse = normalise(inputs[...])
    normed = (unit * vectors[0:1, :] + vectors[2:3, :]).astype(BF16)
    weight_acc[:, : 3 * width] += t_dot(normed, grad_low)
    grad_normed = dot_t(grad_low, qkv_weight[...])
    sums[1:2, :] += column_sum(grad_normed * unit)
    sums[2:3, :] += column_sum(grad_normed)
    total = middle_in[...] + norm_back(grad_normed, unit, inverse, vectors[0:1, :])
    total_low = total.astype(BF16)
    for b in range(BATCH):
        write_image(input_grad, b, total_low[b * ROWS : (b + 1) * ROWS], back)

    @pl.when(step == pl.num_programs(0) - 1)
    def _():
        weight_grad[:, : 4 * width] = weight_acc[...].astype(BF16)


def whole(shape):
    return pl.BlockSpec(shape, lambda i: (0,) * len(shape), pipeline_mode=pl.Buffered(1))


def kept(shape):
    return pl.BlockSpec(shape, lambda i: (0,) * len(shape))


def per_step(*shape):
    return pl.BlockSpec(shape, lambda i: (i,) + (0,) * (len(shape) - 1))


def reduce_owned(grad):
    return lax.psum_scatter(grad, "weight", scatter_dimension=0, tiled=True)


def per_device(
    shards, images, gains, biases, qkv_weight, bias_table, proj_weight, fc1_weight, fc1_bias,
    fc2_weight, rel_index, cotangent,
):
    number, width = images.shape[0], images.shape[-1]
    heads = bias_table.shape[1] * shards
    width_head = width // heads
    hidden_width = fc1_weight.shape[1]
    own = width // shards
    groups = heads // GROUP
    steps = number // BATCH
    rows = BATCH * ROWS
    windows = BATCH * ACROSS * ACROSS

    qkv_full = lax.all_gather(qkv_weight, "weight", axis=0, tiled=True)
    hidden_lines = hidden_width // shards // own
    table_own = bias_table.T.reshape(-1)
    table_lines = -(-table_own.shape[0] // own)
    table_pad = jnp.pad(table_own, (0, table_lines * own - table_own.shape[0]))
    small = jnp.concatenate(
        [gains, biases, fc1_bias.reshape(hidden_lines, own), table_pad.reshape(table_lines, own)]
    )
    small = lax.all_gather(small, "weight", axis=0)
    vectors = small[:, :8].transpose(1, 0, 2).reshape(8, width).astype(F32)
    expand_bias = small[:, 8 : 8 + hidden_lines].reshape(1, hidden_width).astype(F32)
    table = small[:, 8 + hidden_lines :].reshape(shards, -1)[:, : table_own.shape[0]]
    table = table.reshape(heads, SPAN)
    qkv_bias = jnp.concatenate([vectors[4], jnp.zeros_like(vectors[4]), vectors[5]])[None]

    entries = jnp.arange(SPAN, dtype=jnp.int32)
    hot = (rel_index.T.reshape(-1)[None, :] == entries[:, None]).astype(BF16)
    rel_bias = dot(table, hot).reshape(heads, LEN, LEN)
    rel_bias = jnp.pad(rel_bias, ((0, 0), (0, SLOT - LEN), (0, SLOT - LEN)))
    rel_bias = rel_bias.reshape(groups, GROUP * SLOT, SLOT)
    later = jnp.concatenate([fc1_weight, proj_weight], axis=1)
    qkv_full, vectors, expand_bias, rel_bias, later, fc2_weight = lax.optimization_barrier(
        (qkv_full, vectors, expand_bias, rel_bias, later, fc2_weight)
    )
    later = lax.all_gather(later, "weight", axis=0, tiled=True)
    reduce = lax.all_gather(fc2_weight, "weight", axis=0, tiled=True)
    mask = jnp.asarray(region_mask())
    perm_host = token_permutation()
    perm = jnp.asarray(perm_host, BF16)
    back = jnp.asarray(perm_host.T, BF16)

    image_block = per_step(BATCH, GRID, GRID, width)
    shape = jax.ShapeDtypeStruct
    params = pltpu.CompilerParams(
        dimension_semantics=("arbitrary",), vmem_limit_bytes=60 * 1024 * 1024
    )
    tokens = number * ROWS
    mixed, attended, probs = pl.pallas_call(
        functools.partial(attention_kernel, width_head),
        grid=(steps,),
        in_specs=[
            image_block, whole(qkv_full.shape), whole(vectors.shape), whole(qkv_bias.shape),
            whole(rel_bias.shape), whole(mask.shape), whole(perm.shape),
        ],
        out_specs=[
            per_step(rows, 3 * width), per_step(rows, width),
            per_step(windows * groups, GROUP * SLOT, SLOT),
        ],
        out_shape=[
            shape((tokens, 3 * width), BF16), shape((tokens, width), BF16),
            shape((number * ACROSS * ACROSS * groups, GROUP * SLOT, SLOT), BF16),
        ],
        scratch_shapes=[
            pltpu.VMEM((GRID * LINE, width), BF16), pltpu.VMEM((rows, width), F32),
            pltpu.VMEM((rows, 3 * width), F32), pltpu.VMEM((rows, width), F32),
        ],
        compiler_params=params,
        cost_estimate=pl.CostEstimate(flops=60 * 10**9, bytes_accessed=40 * 10**6, transcendentals=0),
    )(images, qkv_full, vectors, qkv_bias, rel_bias, mask, perm)

    output, middle, expand_grad, reduce_grad, sums, expand_sums = pl.pallas_call(
        mlp_kernel,
        grid=(steps,),
        in_specs=[
            image_block, image_block, per_step(rows, width), whole(later.shape), whole(reduce.shape), whole(vectors.shape),
            whole(expand_bias.shape), whole(perm.shape), whole(back.shape),
        ],
        out_specs=[
            image_block, per_step(rows, width), kept((width, hidden_width)),
            kept((hidden_width, width)), kept((8, width)), kept((1, hidden_width)),
        ],
        out_shape=[
            shape(images.shape, BF16), shape((tokens, width), F32),
            shape((width, hidden_width), BF16), shape((hidden_width, width), BF16),
            shape((8, width), F32), shape((1, hidden_width), F32),
        ],
        scratch_shapes=[
            pltpu.VMEM((GRID * LINE, width), BF16), pltpu.VMEM((rows, width), F32),
            pltpu.VMEM((rows, width), F32), pltpu.VMEM((width, hidden_width), F32),
            pltpu.VMEM((hidden_width, width), F32),
        ],
        compiler_params=params,
        cost_estimate=pl.CostEstimate(flops=70 * 10**9, bytes_accessed=40 * 10**6, transcendentals=0),
    )(images, cotangent, attended, later, reduce, vectors, expand_bias, perm, back)

    expand_owned = reduce_owned(expand_grad)
    reduce_owned_grad = reduce_owned(reduce_grad)
    proj_block = pl.BlockSpec(
        (width, width), lambda i: (0, hidden_width // width), pipeline_mode=pl.Buffered(1)
    )

    input_grad, weight_grad, sums_two, mixed_sums, rel_grad = pl.pallas_call(
        functools.partial(backward_kernel, width_head),
        grid=(steps,),
        in_specs=[
            image_block, whole(qkv_full.shape), proj_block, whole(vectors.shape),
            per_step(rows, 3 * width), per_step(rows, width), per_step(rows, width),
            per_step(windows * groups, GROUP * SLOT, SLOT), whole(perm.shape), whole(back.shape),
        ],
        out_specs=[
            image_block, kept((width, 4 * width + own)), kept((8, width)), kept((1, 3 * width)),
            kept((groups, GROUP * SLOT, SLOT)),
        ],
        out_shape=[
            shape(images.shape, BF16), shape((width, 4 * width + own), BF16), shape((8, width), F32),
            shape((1, 3 * width), F32), shape((groups, GROUP * SLOT, SLOT), F32),
        ],
        scratch_shapes=[
            pltpu.VMEM((GRID * LINE, width), BF16), pltpu.VMEM((rows, width), F32),
            pltpu.VMEM((rows, 3 * width), F32), pltpu.VMEM((rows, width), F32),
            pltpu.VMEM((rows, 3 * width), F32), pltpu.VMEM((width, 4 * width), F32),
        ],
        compiler_params=params,
        cost_estimate=pl.CostEstimate(flops=110 * 10**9, bytes_accessed=60 * 10**6, transcendentals=0),
    )(images, qkv_full, later, vectors, mixed, attended, middle, probs, perm, back)

    rel_rows = rel_grad.reshape(heads, SLOT, SLOT)[:, :LEN, :LEN].reshape(heads, LEN * LEN)
    table_grad = lax.dot_general(
        rel_rows, hot.astype(F32), (((1,), (1,)), ((), ())), precision=lax.Precision.HIGHEST
    ).reshape(shards, table_own.shape[0])
    table_grad = jnp.pad(table_grad, ((0, 0), (0, table_lines * own - table_own.shape[0])))
    mixed_lines = mixed_sums.reshape(3, width)
    features = jnp.concatenate(
        [
            sums_two[1:2], sums[0:1], sums_two[2:3], sums[1:2], mixed_lines[0:1], mixed_lines[2:3],
            sums_two[0:1], sums[2:3],
        ]
    )
    small_grad = jnp.concatenate(
        [
            features.reshape(8, shards, own).transpose(1, 0, 2),
            expand_sums.reshape(shards, hidden_lines, own),
            table_grad.reshape(shards, table_lines, own),
        ],
        axis=1,
    )
    small_grad = jnp.pad(small_grad, ((0, 0), (0, own - small_grad.shape[1]), (0, 0)))
    weight_grad = lax.dynamic_update_slice(
        weight_grad, small_grad.reshape(width, own).astype(BF16), (0, 4 * width)
    )
    weight_grad, expand_owned, reduce_owned_grad = lax.optimization_barrier(
        (weight_grad, expand_owned, reduce_owned_grad)
    )
    weight_owned, expand_owned, reduce_owned_grad = lax.psum(
        (reduce_owned(weight_grad), expand_owned, reduce_owned_grad), "replica"
    )
    weight_owned = weight_owned.astype(F32)
    small_owned = weight_owned[:, 4 * width :]
    table_grad = small_owned[8 + hidden_lines : 8 + hidden_lines + table_lines].reshape(-1)
    table_grad = table_grad[: table_own.shape[0]].reshape(-1, SPAN).T
    return (
        output,
        input_grad,
        small_owned[:2],
        small_owned[2:8],
        weight_owned[:, : 3 * width],
        table_grad,
        weight_owned[:, 3 * width : 4 * width],
        expand_owned.astype(F32),
        small_owned[8 : 8 + hidden_lines].reshape(-1),
        reduce_owned_grad.astype(F32),
    )


def solution(mesh):
    in_specs = (
        P(("replica", "weight"), None, None, None),
        P(None, "weight"),
        P(None, "weight"),
        P("weight", None),
        P(None, "weight"),
        P("weight", None),
        P("weight", None),
        P("weight"),
        P("weight", None),
        P(),
        P(("replica", "weight"), None, None, None),
    )
    out_specs = (
        P(("replica", "weight"), None, None, None),
        P(("replica", "weight"), None, None, None),
        P(None, "weight"),
        P(None, "weight"),
        P("weight", None),
        P(None, "weight"),
        P("weight", None),
        P("weight", None),
        P("weight"),
        P("weight", None),
    )
    return jax.shard_map(
        functools.partial(per_device, mesh.shape["weight"]),
        mesh=mesh,
        in_specs=in_specs,
        out_specs=out_specs,
        check_vma=False,
    )
```

```python
import functools

import jax
import jax.numpy as jnp
import numpy as np
from jax import lax
from jax.experimental import pallas as pl
from jax.experimental.pallas import tpu as pltpu
from jax.sharding import PartitionSpec as P

GRID = 14
WIN = 7
SHIFT = 3
ACROSS = GRID // WIN
LEN = WIN * WIN
SLOT = 56
ROWS = ACROSS * ACROSS * SLOT
LINE = 16
SPAN = (2 * WIN - 1) ** 2
GROUP = 4
BATCH = 2
UNROLL = 2
F32 = jnp.float32
BF16 = jnp.bfloat16
EPSILON = 1e-05


def token_permutation():
    matrix = np.zeros((ROWS, GRID * LINE), np.float32)
    for w in range(ACROSS * ACROSS):
        for i in range(LEN):
            row = ((w // ACROSS) * WIN + i // WIN + SHIFT) % GRID
            col = ((w % ACROSS) * WIN + i % WIN + SHIFT) % GRID
            matrix[w * SLOT + i, row * LINE + col] = 1.0
    return matrix


def region_mask():
    places = np.arange(GRID)
    bands = (places >= GRID - WIN).astype(np.int32) + (places >= GRID - SHIFT).astype(np.int32)
    labels = bands[:, None] * 3 + bands[None, :]
    labels = (
        labels.reshape(ACROSS, WIN, ACROSS, WIN)
        .transpose(0, 2, 1, 3)
        .reshape(ACROSS * ACROSS, LEN)
    )
    mask = np.zeros((ACROSS * ACROSS, SLOT, SLOT), np.float32)
    mask[:, :LEN, :LEN] = np.where(labels[:, :, None] == labels[:, None, :], 0.0, -100.0)
    mask[:, LEN:, :] = -1e30
    return mask


def dot(a, b):
    return jnp.dot(a, b, preferred_element_type=F32)


def dot_t(a, b):
    return lax.dot_general(a, b, (((1,), (1,)), ((), ())), preferred_element_type=F32)


def t_dot(a, b):
    return lax.dot_general(a, b, (((0,), (0,)), ((), ())), preferred_element_type=F32)


def normalise(values):
    center = values - jnp.mean(values, axis=-1, keepdims=True)
    spread = jnp.mean(center * center, axis=-1, keepdims=True)
    inverse = lax.rsqrt(spread + EPSILON)
    return center * inverse, inverse


def norm_back(grad, unit, inverse, gain):
    scaled = grad * gain
    return inverse * (
        scaled
        - jnp.mean(scaled, axis=-1, keepdims=True)
        - unit * jnp.mean(scaled * unit, axis=-1, keepdims=True)
    )


def column_sum(values):
    return jnp.sum(values, axis=0, keepdims=True)


def gelu_parts(hidden):
    bell = jnp.exp(hidden * hidden * -0.5)
    step = 1.0 / (1.0 + (0.3275911 * 0.7071067811865476) * jnp.abs(hidden))
    series = step * (
        0.5 * 0.254829592
        + step
        * (
            0.5 * -0.284496736
            + step * (0.5 * 1.421413741 + step * (0.5 * -1.453152027 + step * (0.5 * 1.061405429)))
        )
    )
    tail = series * bell
    below = jnp.where(hidden < 0.0, tail, 1.0 - tail)
    return below, bell * 0.3989422804014327


def head_masks(width_head):
    lanes = lax.broadcasted_iota(jnp.int32, (SLOT, GROUP * width_head), 1)
    return [
        (lanes >= h * width_head) & (lanes < (h + 1) * width_head) for h in range(GROUP)
    ]


def expand(block, masks):
    return jnp.concatenate([jnp.where(m, block, 0.0) for m in masks], axis=0).astype(BF16)


def collect(rows, masks):
    total = jnp.where(masks[0], rows[:SLOT], 0.0)
    for h in range(1, GROUP):
        total = jnp.where(masks[h], rows[h * SLOT : (h + 1) * SLOT], total)
    return total


def read_image(ref, at, grid_ref, perm_ref):
    for r in range(GRID):
        grid_ref[r * LINE : r * LINE + GRID, :] = ref[at, r]
    return dot(perm_ref[...], grid_ref[...])


def write_image(ref, at, values, back_ref):
    lines = dot(back_ref[...], values).astype(BF16)
    for r in range(GRID):
        ref[at, r] = lines[r * LINE : r * LINE + GRID]


def attention_kernel(
    width_head,
    images, qkv_weight, vectors, qkv_bias, rel_bias, mask, perm,
    mixed_out, attended_out, probs_out,
    grid_rows, inputs, mixed, attended,
):
    width = inputs.shape[1]

    @pl.when(pl.program_id(0) == 0)
    def _():
        grid_rows[...] = jnp.zeros_like(grid_rows)

    for b in range(BATCH):
        inputs[b * ROWS : (b + 1) * ROWS, :] = read_image(images, b, grid_rows, perm)
    unit, _ = normalise(inputs[...])
    normed = (unit * vectors[0:1, :] + vectors[2:3, :]).astype(BF16)
    mixed_low = (dot(normed, qkv_weight[...]) + qkv_bias[...]).astype(BF16)
    mixed_out[...] = mixed_low
    mixed[...] = mixed_low.astype(F32)
    scale = width_head ** (-0.5)

    def attend(w, carry):
        masks = head_masks(width_head)
        rows = pl.ds(pl.multiple_of(w * SLOT, 8), SLOT)
        region = mask[lax.rem(w, ACROSS * ACROSS)]
        size = GROUP * width_head
        for g in range(width // size):
            queries = mixed[rows, g * size : (g + 1) * size].astype(BF16)
            keys = expand(mixed[rows, width + g * size : width + (g + 1) * size], masks)
            values = expand(mixed[rows, 2 * width + g * size : 2 * width + (g + 1) * size], masks)
            scores = dot_t(keys, queries) * scale + rel_bias[g]
            scores = scores.reshape(GROUP, SLOT, SLOT) + region[None]
            raised = jnp.exp(scores - jnp.max(scores, axis=1, keepdims=True))
            probs = raised * (1.0 / jnp.sum(raised, axis=1, keepdims=True))
            probs = probs.reshape(GROUP * SLOT, SLOT).astype(BF16)
            probs_out[w * (width // size) + g] = probs
            attended[rows, g * size : (g + 1) * size] = t_dot(probs, values)
        return carry

    lax.fori_loop(0, BATCH * ACROSS * ACROSS, attend, 0, unroll=UNROLL)
    attended_out[...] = attended[...].astype(BF16)


def mlp_kernel(
    images, cotangent, attended, later, reduce, vectors, expand_bias, perm, back,
    output, middle_out, expand_grad, reduce_grad, sums, expand_sums,
    grid_rows, inputs, ups, expand_acc, reduce_acc,
):
    hidden_width = expand_bias.shape[1]
    step = pl.program_id(0)

    @pl.when(step == 0)
    def _():
        grid_rows[...] = jnp.zeros_like(grid_rows)
        expand_acc[...] = jnp.zeros_like(expand_acc)
        reduce_acc[...] = jnp.zeros_like(reduce_acc)
        sums[...] = jnp.zeros_like(sums)
        expand_sums[...] = jnp.zeros_like(expand_sums)

    for b in range(BATCH):
        inputs[b * ROWS : (b + 1) * ROWS, :] = read_image(images, b, grid_rows, perm)
        ups[b * ROWS : (b + 1) * ROWS, :] = read_image(cotangent, b, grid_rows, perm)
    middle = inputs[...] + dot(attended[...], later[:, hidden_width:]) + vectors[6:7, :]
    unit, inverse = normalise(middle)
    normed_two = (unit * vectors[1:2, :] + vectors[3:4, :]).astype(BF16)
    up = ups[...]
    up_low = up.astype(BF16)
    final = middle + vectors[7:8, :]
    grad_normed = jnp.zeros_like(final)
    chunk = 512
    for c in range(hidden_width // chunk):
        part = slice(c * chunk, (c + 1) * chunk)
        expand_part = later[:, part]
        hidden = dot(normed_two, expand_part) + expand_bias[:, part]
        below, density = gelu_parts(hidden)
        activated = (hidden * below).astype(BF16)
        final = final + dot(activated, reduce[part, :])
        grad_act = dot_t(up_low, reduce[part, :])
        grad_hidden = (grad_act * (below + hidden * density)).astype(BF16)
        expand_sums[:, part] += column_sum(grad_hidden.astype(F32))
        expand_acc[:, part] += t_dot(normed_two, grad_hidden)
        reduce_acc[part, :] += t_dot(activated, up_low)
        grad_normed = grad_normed + dot_t(grad_hidden, expand_part)
    sums[0:1, :] += column_sum(grad_normed * unit)
    sums[1:2, :] += column_sum(grad_normed)
    sums[2:3, :] += column_sum(up)
    middle_out[...] = up + norm_back(grad_normed, unit, inverse, vectors[1:2, :])
    final_low = final.astype(BF16)
    for b in range(BATCH):
        write_image(output, b, final_low[b * ROWS : (b + 1) * ROWS], back)

    @pl.when(step == pl.num_programs(0) - 1)
    def _():
        expand_grad[...] = expand_acc[...].astype(BF16)
        reduce_grad[...] = reduce_acc[...].astype(BF16)


def backward_kernel(
    width_head,
    images, qkv_weight, proj_weight, vectors, mixed_in, attended_in, middle_in, probs_in, perm, back,
    input_grad, weight_grad, sums, mixed_sums, rel_grad,
    grid_rows, inputs, mixed, grad_attended, grad_mixed, weight_acc,
):
    width = inputs.shape[1]
    step = pl.program_id(0)

    @pl.when(step == 0)
    def _():
        grid_rows[...] = jnp.zeros_like(grid_rows)
        weight_acc[...] = jnp.zeros_like(weight_acc)
        sums[...] = jnp.zeros_like(sums)
        mixed_sums[...] = jnp.zeros_like(mixed_sums)
        rel_grad[...] = jnp.zeros_like(rel_grad)

    for b in range(BATCH):
        inputs[b * ROWS : (b + 1) * ROWS, :] = read_image(images, b, grid_rows, perm)
    mixed[...] = mixed_in[...].astype(F32)
    middle_low = middle_in[...].astype(BF16)
    weight_acc[:, 3 * width :] += t_dot(attended_in[...], middle_low)
    sums[0:1, :] += column_sum(middle_low.astype(F32))
    grad_attended[...] = dot_t(middle_low, proj_weight[...]).astype(BF16).astype(F32)
    scale = width_head ** (-0.5)

    def attend(w, carry):
        masks = head_masks(width_head)
        rows = pl.ds(pl.multiple_of(w * SLOT, 8), SLOT)
        size = GROUP * width_head
        for g in range(width // size):
            here = slice(g * size, (g + 1) * size)
            queries = mixed[rows, here].astype(BF16)
            keys = expand(mixed[rows, width + g * size : width + (g + 1) * size], masks)
            values = expand(mixed[rows, 2 * width + g * size : 2 * width + (g + 1) * size], masks)
            grad = grad_attended[rows, here].astype(BF16)
            probs_low = probs_in[w * (width // size) + g]
            probs = probs_low.astype(F32).reshape(GROUP, SLOT, SLOT)
            grad_probs = dot_t(values, grad).reshape(GROUP, SLOT, SLOT)
            grad_values = collect(dot(probs_low, grad), masks)
            shift = jnp.sum(probs * grad_probs, axis=1, keepdims=True)
            grad_scores = (probs * (grad_probs - shift)).reshape(GROUP * SLOT, SLOT).astype(BF16)
            rel_grad[g] += grad_scores.astype(F32)
            grad_mixed[rows, here] = scale * t_dot(grad_scores, keys)
            grad_mixed[rows, width + g * size : width + (g + 1) * size] = scale * collect(
                dot(grad_scores, queries), masks
            )
            grad_mixed[rows, 2 * width + g * size : 2 * width + (g + 1) * size] = grad_values
        return carry

    lax.fori_loop(0, BATCH * ACROSS * ACROSS, attend, 0, unroll=UNROLL)

    grad_low = grad_mixed[...].astype(BF16)
    mixed_sums[...] += column_sum(grad_low.astype(F32))
    unit, inverse = normalise(inputs[...])
    normed = (unit * vectors[0:1, :] + vectors[2:3, :]).astype(BF16)
    weight_acc[:, : 3 * width] += t_dot(normed, grad_low)
    grad_normed = dot_t(grad_low, qkv_weight[...])
    sums[1:2, :] += column_sum(grad_normed * unit)
    sums[2:3, :] += column_sum(grad_normed)
    total = middle_in[...] + norm_back(grad_normed, unit, inverse, vectors[0:1, :])
    total_low = total.astype(BF16)
    for b in range(BATCH):
        write_image(input_grad, b, total_low[b * ROWS : (b + 1) * ROWS], back)

    @pl.when(step == pl.num_programs(0) - 1)
    def _():
        weight_grad[:, : 4 * width] = weight_acc[...].astype(BF16)


def whole(shape):
    return pl.BlockSpec(shape, lambda i: (0,) * len(shape), pipeline_mode=pl.Buffered(1))


def kept(shape):
    return pl.BlockSpec(shape, lambda i: (0,) * len(shape))


def per_step(*shape):
    return pl.BlockSpec(shape, lambda i: (i,) + (0,) * (len(shape) - 1))


def reduce_owned(grad):
    return lax.psum_scatter(grad, "weight", scatter_dimension=0, tiled=True)


def owned_sum_kernel(
    grad, other_a, other_b, out_w, out_a, out_b,
    near_slots, near_sums, far_slot, mine, slots_w, slots_a, slots_b, work_w, work_a, work_b,
    group_send, group_arrive, send, arrive,
):
    me = lax.axis_index("replica")
    place = lax.axis_index("weight")

    def bit_of(index, bit):
        return lax.rem(index // (1 << bit), 2)

    def partner(index, bit):
        return index + (1 - 2 * bit_of(index, bit)) * (1 << bit)

    barrier = pltpu.get_barrier_semaphore()
    targets = [{"weight": partner(place, bit)} for bit in range(2)]
    targets += [{"replica": partner(me, bit)} for bit in range(3)]
    for target in targets:
        pl.semaphore_signal(
            barrier, inc=1, device_id=target, device_id_type=pl.DeviceIdType.MESH
        )
    pl.semaphore_wait(barrier, len(targets))

    def remote(source, landing, send_sem, arrive_sem, target):
        copy = pltpu.make_async_remote_copy(
            src_ref=source, dst_ref=landing, send_sem=send_sem, recv_sem=arrive_sem,
            device_id=target, device_id_type=pl.DeviceIdType.MESH,
        )
        copy.start()
        return copy

    height = mine.shape[0]

    def shard(at):
        return grad.at[pl.ds(pl.multiple_of(at * height, height), height)]

    core, chip = bit_of(place, 0), bit_of(place, 1)
    copies = [
        remote(
            shard(2 * x + 1 - core), near_slots.at[x], group_send.at[x], group_arrive.at[x], targets[0]
        )
        for x in range(2)
    ]
    for x in range(2):
        copies[x].wait()
        near_sums[x] = (
            shard(2 * x + core)[...].astype(F32) + near_slots[x].astype(F32)
        ).astype(BF16)
    copy = remote(near_sums.at[1 - chip], far_slot, group_send.at[2], group_arrive.at[2], targets[1])
    copy.wait()
    mine[...] = (near_sums[chip].astype(F32) + far_slot[...].astype(F32)).astype(BF16)

    sources = (mine, other_a, other_b)
    outs = (out_w, out_a, out_b)
    slots = (slots_w, slots_a, slots_b)
    works = (work_w, work_a, work_b)
    orders = ((0, 1, 2), (1, 0, 2))
    bases = []
    for order in orders:
        base = [0 * me]
        for s, bit in enumerate(order):
            base.append(base[-1] + bit_of(me, bit) * (4 >> s))
        bases.append(base)

    def block(ref, half, first, chunks):
        size = ref.shape[0] // 8
        columns = (ref.shape[1] // 256) * 128
        rows = pl.ds(pl.multiple_of(first * size, size), chunks * size)
        if half == 0:
            return ref.at[rows, :columns]
        return ref.at[rows, columns:]

    def start_sum(s, half):
        bit = orders[half][s]
        chunks = 4 >> s
        away = bases[half][s] + (1 - bit_of(me, bit)) * chunks
        begin = sum(4 >> k for k in range(s))
        return [
            remote(
                block(sources[a] if s == 0 else works[a], half, away, chunks),
                block(slots[a], half, begin, chunks),
                send.at[0, s, half, a], arrive.at[0, s, half, a], targets[2 + bit],
            )
            for a in range(3)
        ]

    def end_sum(s, half, copies):
        chunks = 4 >> s
        begin = sum(4 >> k for k in range(s))
        for a in range(3):
            copies[a].wait()
            held = block(sources[a] if s == 0 else works[a], half, bases[half][s + 1], chunks)
            total = held[...].astype(F32) + block(slots[a], half, begin, chunks)[...].astype(F32)
            kept_in = outs[a] if s == 2 else works[a]
            block(kept_in, half, bases[half][s + 1], chunks)[...] = total.astype(BF16)

    def start_share(s, half):
        bit = orders[half][s]
        chunks = 4 >> s
        return [
            remote(
                block(outs[a], half, bases[half][s + 1], chunks),
                block(outs[a], half, bases[half][s + 1], chunks),
                send.at[1, s, half, a], arrive.at[1, s, half, a], targets[2 + bit],
            )
            for a in range(3)
        ]

    flying = [start_sum(0, 0), start_sum(0, 1)]
    for s in range(3):
        for half in range(2):
            end_sum(s, half, flying[half])
            flying[half] = start_sum(s + 1, half) if s < 2 else start_share(2, half)
    for s in (2, 1, 0):
        for half in range(2):
            for copy in flying[half]:
                copy.wait()
            if s > 0:
                flying[half] = start_share(s - 1, half)


def owned_sums(grad, others, shards, replicas):
    if shards != 4 or replicas != 8:
        return lax.psum((reduce_owned(grad),) + others, "replica")
    height = grad.shape[0] // shards
    shapes = [(height, grad.shape[1])] + [other.shape for other in others]
    vmem = pl.BlockSpec(memory_space=pltpu.VMEM)
    return pl.pallas_call(
        owned_sum_kernel,
        in_specs=[vmem] * 3,
        out_specs=[vmem] * 3,
        out_shape=[jax.ShapeDtypeStruct(shape, BF16) for shape in shapes],
        scratch_shapes=[
            pltpu.VMEM((2,) + shapes[0], BF16), pltpu.VMEM((2,) + shapes[0], BF16),
            pltpu.VMEM(shapes[0], BF16), pltpu.VMEM(shapes[0], BF16),
        ]
        + [pltpu.VMEM(shape, BF16) for shape in shapes] * 2
        + [pltpu.SemaphoreType.DMA((3,))] * 2
        + [pltpu.SemaphoreType.DMA((2, 3, 2, 3))] * 2,
        compiler_params=pltpu.CompilerParams(
            collective_id=0, has_side_effects=True, vmem_limit_bytes=32 * 1024 * 1024
        ),
    )(grad, *others)


def per_device(
    shards, replicas, images, gains, biases, qkv_weight, bias_table, proj_weight, fc1_weight, fc1_bias,
    fc2_weight, rel_index, cotangent,
):
    number, width = images.shape[0], images.shape[-1]
    heads = bias_table.shape[1] * shards
    width_head = width // heads
    hidden_width = fc1_weight.shape[1]
    own = width // shards
    groups = heads // GROUP
    steps = number // BATCH
    rows = BATCH * ROWS
    windows = BATCH * ACROSS * ACROSS

    qkv_full = lax.all_gather(qkv_weight, "weight", axis=0, tiled=True)
    hidden_lines = hidden_width // shards // own
    table_own = bias_table.T.reshape(-1)
    table_lines = -(-table_own.shape[0] // own)
    table_pad = jnp.pad(table_own, (0, table_lines * own - table_own.shape[0]))
    small = jnp.concatenate(
        [gains, biases, fc1_bias.reshape(hidden_lines, own), table_pad.reshape(table_lines, own)]
    )
    small = lax.all_gather(small, "weight", axis=0)
    vectors = small[:, :8].transpose(1, 0, 2).reshape(8, width).astype(F32)
    expand_bias = small[:, 8 : 8 + hidden_lines].reshape(1, hidden_width).astype(F32)
    table = small[:, 8 + hidden_lines :].reshape(shards, -1)[:, : table_own.shape[0]]
    table = table.reshape(heads, SPAN)
    qkv_bias = jnp.concatenate([vectors[4], jnp.zeros_like(vectors[4]), vectors[5]])[None]

    entries = jnp.arange(SPAN, dtype=jnp.int32)
    hot = (rel_index.T.reshape(-1)[None, :] == entries[:, None]).astype(BF16)
    rel_bias = dot(table, hot).reshape(heads, LEN, LEN)
    rel_bias = jnp.pad(rel_bias, ((0, 0), (0, SLOT - LEN), (0, SLOT - LEN)))
    rel_bias = rel_bias.reshape(groups, GROUP * SLOT, SLOT)
    later = jnp.concatenate([fc1_weight, proj_weight], axis=1)
    qkv_full, vectors, expand_bias, rel_bias, later, fc2_weight = lax.optimization_barrier(
        (qkv_full, vectors, expand_bias, rel_bias, later, fc2_weight)
    )
    later = lax.all_gather(later, "weight", axis=0, tiled=True)
    reduce = lax.all_gather(fc2_weight, "weight", axis=0, tiled=True)
    mask = jnp.asarray(region_mask())
    perm_host = token_permutation()
    perm = jnp.asarray(perm_host, BF16)
    back = jnp.asarray(perm_host.T, BF16)

    image_block = per_step(BATCH, GRID, GRID, width)
    shape = jax.ShapeDtypeStruct
    params = pltpu.CompilerParams(
        dimension_semantics=("arbitrary",), vmem_limit_bytes=60 * 1024 * 1024
    )
    tokens = number * ROWS
    mixed, attended, probs = pl.pallas_call(
        functools.partial(attention_kernel, width_head),
        grid=(steps,),
        in_specs=[
            image_block, whole(qkv_full.shape), whole(vectors.shape), whole(qkv_bias.shape),
            whole(rel_bias.shape), whole(mask.shape), whole(perm.shape),
        ],
        out_specs=[
            per_step(rows, 3 * width), per_step(rows, width),
            per_step(windows * groups, GROUP * SLOT, SLOT),
        ],
        out_shape=[
            shape((tokens, 3 * width), BF16), shape((tokens, width), BF16),
            shape((number * ACROSS * ACROSS * groups, GROUP * SLOT, SLOT), BF16),
        ],
        scratch_shapes=[
            pltpu.VMEM((GRID * LINE, width), BF16), pltpu.VMEM((rows, width), F32),
            pltpu.VMEM((rows, 3 * width), F32), pltpu.VMEM((rows, width), F32),
        ],
        compiler_params=params,
        cost_estimate=pl.CostEstimate(flops=60 * 10**9, bytes_accessed=40 * 10**6, transcendentals=0),
    )(images, qkv_full, vectors, qkv_bias, rel_bias, mask, perm)

    output, middle, expand_grad, reduce_grad, sums, expand_sums = pl.pallas_call(
        mlp_kernel,
        grid=(steps,),
        in_specs=[
            image_block, image_block, per_step(rows, width), whole(later.shape), whole(reduce.shape), whole(vectors.shape),
            whole(expand_bias.shape), whole(perm.shape), whole(back.shape),
        ],
        out_specs=[
            image_block, per_step(rows, width), kept((width, hidden_width)),
            kept((hidden_width, width)), kept((8, width)), kept((1, hidden_width)),
        ],
        out_shape=[
            shape(images.shape, BF16), shape((tokens, width), F32),
            shape((width, hidden_width), BF16), shape((hidden_width, width), BF16),
            shape((8, width), F32), shape((1, hidden_width), F32),
        ],
        scratch_shapes=[
            pltpu.VMEM((GRID * LINE, width), BF16), pltpu.VMEM((rows, width), F32),
            pltpu.VMEM((rows, width), F32), pltpu.VMEM((width, hidden_width), F32),
            pltpu.VMEM((hidden_width, width), F32),
        ],
        compiler_params=params,
        cost_estimate=pl.CostEstimate(flops=70 * 10**9, bytes_accessed=40 * 10**6, transcendentals=0),
    )(images, cotangent, attended, later, reduce, vectors, expand_bias, perm, back)

    expand_owned = reduce_owned(expand_grad)
    reduce_owned_grad = reduce_owned(reduce_grad)
    proj_block = pl.BlockSpec(
        (width, width), lambda i: (0, hidden_width // width), pipeline_mode=pl.Buffered(1)
    )

    input_grad, weight_grad, sums_two, mixed_sums, rel_grad = pl.pallas_call(
        functools.partial(backward_kernel, width_head),
        grid=(steps,),
        in_specs=[
            image_block, whole(qkv_full.shape), proj_block, whole(vectors.shape),
            per_step(rows, 3 * width), per_step(rows, width), per_step(rows, width),
            per_step(windows * groups, GROUP * SLOT, SLOT), whole(perm.shape), whole(back.shape),
        ],
        out_specs=[
            image_block, kept((width, 4 * width + own)), kept((8, width)), kept((1, 3 * width)),
            kept((groups, GROUP * SLOT, SLOT)),
        ],
        out_shape=[
            shape(images.shape, BF16), shape((width, 4 * width + own), BF16), shape((8, width), F32),
            shape((1, 3 * width), F32), shape((groups, GROUP * SLOT, SLOT), F32),
        ],
        scratch_shapes=[
            pltpu.VMEM((GRID * LINE, width), BF16), pltpu.VMEM((rows, width), F32),
            pltpu.VMEM((rows, 3 * width), F32), pltpu.VMEM((rows, width), F32),
            pltpu.VMEM((rows, 3 * width), F32), pltpu.VMEM((width, 4 * width), F32),
        ],
        compiler_params=params,
        cost_estimate=pl.CostEstimate(flops=110 * 10**9, bytes_accessed=60 * 10**6, transcendentals=0),
    )(images, qkv_full, later, vectors, mixed, attended, middle, probs, perm, back)

    rel_rows = rel_grad.reshape(heads, SLOT, SLOT)[:, :LEN, :LEN].reshape(heads, LEN * LEN)
    table_grad = lax.dot_general(
        rel_rows, hot.astype(F32), (((1,), (1,)), ((), ())), precision=lax.Precision.HIGHEST
    ).reshape(shards, table_own.shape[0])
    table_grad = jnp.pad(table_grad, ((0, 0), (0, table_lines * own - table_own.shape[0])))
    mixed_lines = mixed_sums.reshape(3, width)
    features = jnp.concatenate(
        [
            sums_two[1:2], sums[0:1], sums_two[2:3], sums[1:2], mixed_lines[0:1], mixed_lines[2:3],
            sums_two[0:1], sums[2:3],
        ]
    )
    small_grad = jnp.concatenate(
        [
            features.reshape(8, shards, own).transpose(1, 0, 2),
            expand_sums.reshape(shards, hidden_lines, own),
            table_grad.reshape(shards, table_lines, own),
        ],
        axis=1,
    )
    small_grad = jnp.pad(small_grad, ((0, 0), (0, own - small_grad.shape[1]), (0, 0)))
    weight_grad = lax.dynamic_update_slice(
        weight_grad, small_grad.reshape(width, own).astype(BF16), (0, 4 * width)
    )
    weight_grad, expand_owned, reduce_owned_grad = lax.optimization_barrier(
        (weight_grad, expand_owned, reduce_owned_grad)
    )
    weight_owned, expand_owned, reduce_owned_grad = owned_sums(
        weight_grad, (expand_owned, reduce_owned_grad), shards, replicas
    )
    weight_owned = weight_owned.astype(F32)
    small_owned = weight_owned[:, 4 * width :]
    table_grad = small_owned[8 + hidden_lines : 8 + hidden_lines + table_lines].reshape(-1)
    table_grad = table_grad[: table_own.shape[0]].reshape(-1, SPAN).T
    return (
        output,
        input_grad,
        small_owned[:2],
        small_owned[2:8],
        weight_owned[:, : 3 * width],
        table_grad,
        weight_owned[:, 3 * width : 4 * width],
        expand_owned.astype(F32),
        small_owned[8 : 8 + hidden_lines].reshape(-1),
        reduce_owned_grad.astype(F32),
    )


def solution(mesh):
    in_specs = (
        P(("replica", "weight"), None, None, None),
        P(None, "weight"),
        P(None, "weight"),
        P("weight", None),
        P(None, "weight"),
        P("weight", None),
        P("weight", None),
        P("weight"),
        P("weight", None),
        P(),
        P(("replica", "weight"), None, None, None),
    )
    out_specs = (
        P(("replica", "weight"), None, None, None),
        P(("replica", "weight"), None, None, None),
        P(None, "weight"),
        P(None, "weight"),
        P("weight", None),
        P(None, "weight"),
        P("weight", None),
        P("weight", None),
        P("weight"),
        P("weight", None),
    )
    return jax.shard_map(
        functools.partial(per_device, mesh.shape["weight"], mesh.shape["replica"]),
        mesh=mesh,
        in_specs=in_specs,
        out_specs=out_specs,
        check_vma=False,
    )
```
